32 devices in a mesh: groups: 2 (over y), beam: 4 (over z), angle: 2 (over core), trans: 2 (over x).
Axes of the slice: x: 2, y: 2, z: 4, core: 2. Of those that a mesh axis runs over, the one named last changes fastest.
Arguments:
- density: float32 [4, 8, 128, 512], P(None, 'groups', 'beam', 'trans'), parts along dimension 1, may hold values from 0.2 to 1.5
- measured: float32 [4, 8, 4, 512], P('angle', 'groups', None, 'trans'), parts along dimension 1, may hold values from -3 to 3
- offsets: int32 [4], P('angle'), may hold values from -4 to 3, as said below
- sides: int32 [4], P('angle'), may hold values from 0 to 1, as said below
- shear_frac: float32 [4], P('angle'), may hold values from 0.1 to 0.9
- k_incident: float32 [4], replicated, may hold values from 0.5 to 3
- k_fluor: float32 [4, 4], replicated, may hold values from 0.2 to 2
Outputs:
- updated: float32 [4, 8, 128, 512], P(None, ('groups', 'angle'), 'beam', 'trans'), parts along dimension 1
- residual: float32 [4, 8, 4, 512], P('angle', 'groups', None, 'trans'), parts along dimension 1
The draws below stay inside these ranges and needn't reach their ends.
There are 2 independent parts, one for each index of `groups`. The reference program is written for one: setup_inputs(seed, part) draws one part's arguments, and reference() takes and returns one part's arrays. A program takes and returns all parts, laid end to end along the dimension named above; an argument that names none is the same for every part. Nothing has to cross between parts.
Inputs may be any that keep to these rules, and one draw needn't show every extreme that they name: `offsets`: each offset lies in -4 to 3, and both ends occur among the angles. `sides`: exactly half of the angles, rounded down, have detector side 1.
All inputs are finite; a program needn't handle non-finite values.
Results may differ from the reference program's by a relative error of at most 0.0003.
Values sent between devices are 32-bit elements; how exact they have to be, the bound alone decides.
A program may use at most 64 MiB of HBM per device.

```python
import math
import jax
import jax.numpy as jnp
from jax import lax

E = 4
S = 4
HALO = 4
NB = 128
NT = 512
ANGLES = 4


def draw_offsets(key, part):
    base = jax.random.randint(key, (ANGLES,), -HALO, HALO).astype(jnp.int32)
    order = jax.random.permutation(jax.random.fold_in(key, 1), ANGLES)
    base = base.at[order[0]].set(-HALO)
    base = base.at[order[1]].set(HALO - 1)
    return base.astype(jnp.int32)


def draw_sides(key, part):
    order = jax.random.permutation(jax.random.fold_in(key, 7), ANGLES).astype(jnp.int32)
    return jnp.where(order < ANGLES // 2, 1, 0).astype(jnp.int32)


def block_levels(rng, shape, cuts, low, top_value):
    factor_of, own = 1.0, jax.random.fold_in(rng, 6)
    for position, parts in cuts:
        steps = jnp.exp(jax.random.uniform(jax.random.fold_in(own, position), (parts,), jnp.float32, low / len(cuts), top_value / len(cuts)))
        factor_of = factor_of * jnp.repeat(steps, shape[position] // parts).reshape([-1 if axis == position else 1 for axis in range(len(shape))])
    return factor_of


def scatter_about(stream_key, shape, spread, limit, cuts=(), kind=jnp.bfloat16):
    entries = jax.random.normal(stream_key, shape, jnp.float32) * spread
    if len(cuts) > 0:
        entries = block_levels(stream_key, shape, cuts, -0.22, 0.18) * entries
    return jnp.clip(entries, min=-limit, max=limit).astype(kind)


def setup_inputs(seed: int = 0, part: int = 0) -> dict:
    splits = jax.random.split(jax.random.key(seed), 8)
    own_keys = jax.random.split(jax.random.fold_in(splits[7], part), 8)
    return {
        "density": jnp.clip(0.2 + 1.3 * jax.random.uniform(own_keys[0], (E, S, NB, NT), jnp.float32) ** block_levels(own_keys[0], (E, S, NB, NT), ((2, 4), (3, 2)), -0.2, 0.2), 0.2, 1.5),
        "measured": scatter_about(own_keys[1], (ANGLES, S, E, NT), 0.2, 3.0, ((0, 2), (3, 2)), jnp.float32),
        "offsets": draw_offsets(jax.random.fold_in(splits[7], 71), part),
        "sides": draw_sides(jax.random.fold_in(splits[7], 71), part),
        "shear_frac": jnp.clip(0.1 + 0.79999997 * jax.random.uniform(splits[4], (ANGLES,), jnp.float32) ** block_levels(splits[4], (ANGLES,), ((0, 2),), -0.2, 0.2), 0.1, 0.9),
        "k_incident": jnp.clip(jnp.exp(jax.random.uniform(splits[5], (E,), jnp.float32, math.log(0.5), math.log(3.0))), 0.5, 3.0),
        "k_fluor": jnp.clip(jnp.exp(jax.random.uniform(splits[6], (E, E), jnp.float32, math.log(0.2), math.log(2.0))), 0.2, 2.0),
    }


def forward_angle(rho, offset, frac, side, k_incident, k_fluor):
    padded = jnp.pad(rho, ((0, 0), (0, 0), (0, 0), (HALO, HALO)))
    start = (HALO + offset).astype(jnp.int32)
    lower = lax.dynamic_slice_in_dim(padded, start, NT, 3)
    upper = lax.dynamic_slice_in_dim(padded, start + 1, NT, 3)
    sheared = (1.0 - frac) * lower + frac * upper
    atten = jnp.einsum('e,esbt->sbt', k_incident, sheared, precision=lax.Precision.HIGHEST)
    incident = jnp.exp(-(0.5 / NB) * (jnp.cumsum(atten, axis=1) - 0.5 * atten))
    fluor = jnp.einsum('ef,fsbt->esbt', k_fluor, sheared, precision=lax.Precision.HIGHEST)
    running = jnp.cumsum(fluor, axis=3)
    before = running - fluor
    after = running[..., -1:] - running
    path = 0.5 / NT * (jnp.where(side == 1, after, before) + 0.5 * fluor)
    signal = 0.5 / NB * lax.optimization_barrier(jnp.sum(sheared * incident[None] * jnp.exp(-path), axis=2))
    return jnp.transpose(signal, (1, 0, 2))

def reference(density, measured, offsets, sides, shear_frac, k_incident, k_fluor):

    def one(total, items):
        offset, frac, side, observed = items
        signal, pullback = jax.vjp(lambda rho: forward_angle(rho, offset, frac, side, k_incident, k_fluor), density)
        missed = signal - observed
        grad = pullback(missed)[0]
        return (total + grad, missed)
    total_grad, residual = lax.scan(one, jnp.zeros_like(density), (offsets, shear_frac, sides, measured))
    updated = density - 8.0 * NB / ANGLES * total_grad
    return (updated, residual)
```

```python
import functools

import jax
import jax.numpy as jnp
from jax import lax
from jax.experimental import pallas as pl
from jax.experimental.pallas import tpu as pltpu
from jax.sharding import PartitionSpec as P

F32 = jnp.float32
BF16 = jnp.bfloat16
FAR = 1 << 20
HALO = 4
ROWS = 8


def split(x):
    hi = x.astype(BF16)
    return hi, (x - hi.astype(F32)).astype(BF16)


def nn(a, b):
    return lax.dot_general(a, b, (((1,), (0,)), ((), ())), preferred_element_type=F32)


def nt(a, b):
    return lax.dot_general(a, b, (((1,), (1,)), ((), ())), preferred_element_type=F32)


def iota(shape, dim):
    return lax.broadcasted_iota(jnp.int32, shape, dim)


def two_taps(at_zero, at_one, frac):
    keep = jnp.full((1, at_zero.shape[1]), 1.0 - frac, F32)
    take = jnp.full((1, at_zero.shape[1]), frac, F32)
    keep_hi = keep.astype(BF16).astype(F32)
    take_hi = take.astype(BF16).astype(F32)
    hi = jnp.where(at_zero, keep_hi, jnp.where(at_one, take_hi, 0.0))
    lo = jnp.where(at_zero, keep - keep_hi, jnp.where(at_one, take - take_hi, 0.0))
    return hi.astype(BF16), lo.astype(BF16)


def stack_t(x):
    hi = x.astype(BF16).astype(F32)
    rows = x.shape[0]
    full = -(-3 * rows // 128) * 128
    parts = [hi, x - hi, hi]
    if full > 3 * rows:
        parts.append(jnp.zeros((full - 3 * rows, x.shape[1]), F32))
    return jnp.transpose(jnp.concatenate(parts, axis=0)).astype(BF16)


def stack_w(hi, lo):
    rows = hi.shape[0]
    full = -(-3 * rows // 128) * 128
    parts = [hi.astype(F32), hi.astype(F32), lo.astype(F32)]
    if full > 3 * rows:
        parts.append(jnp.zeros((full - 3 * rows, hi.shape[1]), F32))
    return jnp.concatenate(parts, axis=0).astype(BF16)


def kernel(sizes, dens, meas, offs, sides, fracs, kinc, kfl, upd, res,
           gsend, gbuf, kbuf, pbuf, pabuf, wt, wsd, rsend, rbuf, gmain, mrecv,
           m_hi, m_lo, tri, gs_s, gr_s, ks_s, kr_s, ps_s, pr_s, as_s, ar_s, ms_s, mr_s, rs_s, rr_s):
    nb, na, nx = sizes
    elems, slices, cells, width = dens.shape
    angles = meas.shape[0]
    share = slices // na
    unit = share * cells
    rows_h = elems * unit
    beam_total = cells * nb
    trans_total = width * nx
    dxb = 0.5 / beam_total
    dxt = 0.5 / trans_total
    half = width // 2
    grp = lax.axis_index("groups")
    me_b = lax.axis_index("beam")
    me_a = lax.axis_index("angle")
    me_x = lax.axis_index("trans")

    def dev(b, a, x):
        return (grp, b, a, x)

    def peers(me, count):
        return [lax.rem(me + k, count) for k in range(1, count)]

    barrier = pltpu.get_barrier_semaphore()
    greeted = 0
    for kb in range(nb):
        for kx in range(nx):
            if kb or kx:
                pl.semaphore_signal(barrier, inc=1, device_id_type=pl.DeviceIdType.MESH,
                                    device_id=dev(lax.rem(me_b + kb, nb), me_a, lax.rem(me_x + kx, nx)))
                greeted += 1
    for ka in range(1, na):
        for kx in range(nx):
            pl.semaphore_signal(barrier, inc=1, device_id_type=pl.DeviceIdType.MESH,
                                device_id=dev(me_b, lax.rem(me_a + ka, na), lax.rem(me_x + kx, nx)))
            greeted += 1

    def send(src, dst, ssem, rsem, to):
        copy = pltpu.make_async_remote_copy(src_ref=src, dst_ref=dst, send_sem=ssem, recv_sem=rsem,
                                            device_id=to, device_id_type=pl.DeviceIdType.MESH)
        copy.start()
        return copy

    def arrive(dst, ssem, rsem):
        pltpu.make_async_remote_copy(src_ref=dst, dst_ref=dst, send_sem=ssem, recv_sem=rsem,
                                     device_id=dev(me_b, me_a, me_x),
                                     device_id_type=pl.DeviceIdType.MESH).wait_recv()

    sent = []
    off = [offs[a] for a in range(angles)]
    side = [sides[a] for a in range(angles)]
    frac = [fracs[a] for a in range(angles)]

    def dens_rows(h, e):
        return dens[e, pl.ds(h * share, share)].reshape(unit, width)

    q = iota((2 * ROWS, width), 0)
    u = iota((2 * ROWS, width), 1)
    up = q < ROWS
    qq = jnp.where(up, q, q - ROWS)
    pick = jnp.where((qq < HALO) & (jnp.where(up, width - HALO + qq, qq) == u), 1.0, 0.0)
    e_hi, e_lo = pick.astype(BF16).astype(F32), jnp.zeros_like(pick)

    def counted(t):
        inside = (t + me_x * width >= 0) & (t + me_x * width < trans_total)
        kept = jnp.where(up, t, width - 1 - t) < width
        return kept & inside, jnp.logical_not(kept) & inside

    for a in range(angles):
        t0 = u - off[a]
        in0, out0 = counted(t0)
        in1, out1 = counted(t0 - 1)
        keep = jnp.full((1, width), 1.0 - frac[a], F32)
        take = jnp.full((1, width), frac[a], F32)
        val_in = jnp.where(in0, keep, 0.0) + jnp.where(in1, take, 0.0)
        val_out = jnp.where(out0, keep, 0.0) + jnp.where(out1, take, 0.0)
        val = jnp.where(qq == HALO + a, val_in, jnp.where(qq == HALO + angles + a, val_out, 0.0))
        val_hi = val.astype(BF16).astype(F32)
        e_hi = e_hi + val_hi
        e_lo = e_lo + (val - val_hi)
    e_both = jnp.concatenate([e_hi, e_lo], axis=0).astype(BF16)
    e_hi = e_hi.astype(BF16)

    total = sum(kinc[e] * dens[e] for e in range(elems))
    ksum = jnp.sum(total, axis=1)
    k8 = jnp.concatenate([ksum[:, :half], ksum[:, half:]], axis=0)
    kbuf[me_b * nx + me_x] = k8
    dhl = []
    for h in range(na):
        d = jnp.concatenate([dens_rows(h, e) for e in range(elems)], axis=0)
        d_hi, d_lo = split(d)
        dhl.append((d_hi, d_lo))
        first = nt(e_both, d_hi)
        msg = first[: 2 * ROWS] + first[2 * ROWS :] + nt(e_hi, d_lo)
        gsend[:, h * rows_h : (h + 1) * rows_h] = msg
    prm = iota((ROWS, 128), 0)
    tile = jnp.zeros((ROWS, 128), F32)
    for a in range(angles):
        tile = jnp.where(prm == 3 * a, off[a].astype(F32), tile)
        tile = jnp.where(prm == 3 * a + 1, frac[a], tile)
        tile = jnp.where(prm == 3 * a + 2, side[a].astype(F32), tile)
    pabuf[me_a] = tile

    pl.semaphore_wait(barrier, greeted)
    for x in peers(me_x, nx):
        part = pl.multiple_of(jnp.where(x > me_x, 0, ROWS), ROWS)
        sent.append(send(gsend.at[pl.ds(part, ROWS)], gbuf.at[me_x], gs_s.at[x], gr_s.at[me_x], dev(me_b, me_a, x)))
    for kb in range(1, nb):
        for kx in range(nx):
            b, x = lax.rem(me_b + kb, nb), lax.rem(me_x + kx, nx)
            own = kbuf.at[me_b * nx + me_x]
            sent.append(send(own, own, ks_s.at[b * nx + x], kr_s.at[me_b * nx + me_x], dev(b, me_a, x)))
    for a in peers(me_a, na):
        own = pabuf.at[me_a]
        sent.append(send(own, own, as_s.at[a], ar_s.at[me_a], dev(me_b, a, me_x)))

    k = iota((width + 128, width), 0)
    t = iota((width + 128, width), 1)
    col = jnp.where(k < width + 64, k, k - width - 128)
    d0 = col - t
    td = iota((width, width), 0) - iota((width, width), 1)
    for a in range(angles):
        hi, lo = two_taps(d0 == off[a], d0 == off[a] + 1, frac[a])
        m_hi[a] = hi
        m_lo[a] = lo
        sgn = jnp.where(side[a] == 1, 1, -1)
        tri[a] = jnp.where(td == 0, 0.5, jnp.where(td * sgn > 0, 1.0, 0.0)).astype(BF16)
    r0 = iota((unit, unit), 0)
    r1 = iota((unit, unit), 1)
    same = (r0 // cells) == (r1 // cells)
    low = jnp.where(r0 == r1, 0.5, jnp.where(same & (r1 < r0), 1.0, 0.0)).astype(BF16)
    high = jnp.where(r0 == r1, 0.5, jnp.where(same & (r1 > r0), 1.0, 0.0)).astype(BF16)
    g = iota((ROWS * nx, width), 0)
    gt = iota((ROWS * nx, width), 1)
    gx = g // ROWS
    gq = g - gx * ROWS
    gcol = jnp.where(gx == me_x + 1, width + gq, jnp.where(gx == me_x - 1, gq - HALO, FAR))
    gcol = jnp.where(gq < HALO, gcol, FAR)
    halo_w = []
    for a in range(angles):
        hi, lo = two_taps(gcol - gt == off[a], gcol - gt == off[a] + 1, frac[a])
        seen = jnp.where(side[a] == 1, gx - me_x, me_x - gx)
        use = ((gq == HALO + a) & (seen > 0)) | ((gq == HALO + angles + a) & ((seen == 0) | (seen > 1)))
        ca = jnp.where(use, 1.0, 0.0).astype(BF16)
        halo_w.append((stack_w(hi, lo), stack_w(ca, jnp.zeros_like(ca))))

    sheared0 = [[nn(dhl[h][0], m_hi[a, :width]) + nn(dhl[h][1], m_hi[a, :width]) + nn(dhl[h][0], m_lo[a, :width])
                 for a in range(angles)] for h in range(na)]

    spill = gsend[...]
    own_slot = spill[:ROWS]
    sq = iota((ROWS, spill.shape[1]), 0)
    for a in range(angles):
        pick_up = jnp.where(side[a] == 1, 1, 0)
        chosen = jnp.where((sq == HALO + angles + a) & (pick_up == 0), spill[ROWS:], own_slot)
        own_slot = chosen
    gbuf[me_x] = own_slot

    for x in peers(me_x, nx):
        arrive(gbuf.at[x], gs_s.at[x], gr_s.at[x])
    for kb in range(1, nb):
        for kx in range(nx):
            i = lax.rem(me_b + kb, nb) * nx + lax.rem(me_x + kx, nx)
            arrive(kbuf.at[i], ks_s.at[i], kr_s.at[i])

    ups = []
    for x in range(nx):
        acc = jnp.zeros((2 * slices, half), F32)
        for b in range(nb):
            acc = acc + jnp.where(b < me_b, kbuf[b * nx + x], 0.0)
        ups.append(acc)
    own_up = sum(jnp.where(me_x == x, ups[x], 0.0) for x in range(nx))
    right = sum(jnp.where(me_x + 1 == x, ups[x], 0.0) for x in range(nx))
    left = sum(jnp.where(me_x - 1 == x, ups[x], 0.0) for x in range(nx))
    lane = iota((slices, half), 1)
    rim = jnp.where(lane < 64, right[:slices], left[slices:])
    kext = jnp.concatenate([own_up[:slices], own_up[slices:], rim], axis=1)
    kext = jnp.concatenate([kext, jnp.zeros_like(kext)], axis=0)
    k_hi, k_lo = split(kext)
    carried = [nn(k_hi, m_hi[a]) + nn(k_lo, m_hi[a]) + nn(k_hi, m_lo[a]) for a in range(angles)]

    gall = jnp.concatenate([gbuf[x] for x in range(nx)], axis=0)
    g_t = stack_t(gall)

    def spread_rows(rows):
        return jnp.broadcast_to(rows[:, None, :], (share, cells, width)).reshape(unit, width)

    for h in range(na):
        gh = g_t[h * rows_h : (h + 1) * rows_h]
        for a in range(angles):
            x = sheared0[h][a] + nn(gh, halo_w[a][0])
            x_hi, x_lo = split(x)
            raw = nn(x_hi, tri[a]) + nn(x_lo, tri[a]) + nn(gh, halo_w[a][1])
            atten = sum(kinc[e] * x[e * unit : (e + 1) * unit] for e in range(elems))
            a_hi, a_lo = split(atten)
            inc = dxb * (nn(low, a_hi) + nn(low, a_lo) + spread_rows(carried[a][h * share : (h + 1) * share]))
            for e in range(elems):
                path = inc
                for f in range(elems):
                    path = path + (dxt * kfl[e, f]) * raw[f * unit : (f + 1) * unit]
                w = dxb * jnp.exp(-path)
                ws = w * x[e * unit : (e + 1) * unit]
                wt[h, a, e] = w
                wsd[h, a, e] = ws
                part = jnp.sum(ws.reshape(share, cells, width), axis=1)
                for s in range(share):
                    row = (a * share + s) * elems + e
                    pbuf[me_b, h, row : row + 1] = part[s : s + 1]
        for b in peers(me_b, nb):
            own = pbuf.at[me_b, h]
            sent.append(send(own, own, ps_s.at[h * nb + b], pr_s.at[h * nb + me_b], dev(b, me_a, me_x)))

    for a in peers(me_a, na):
        arrive(pabuf.at[a], as_s.at[a], ar_s.at[a])
    rq = iota((2 * ROWS, width), 0)
    rt = iota((2 * ROWS, width), 1)
    rcol = jnp.where(rq < HALO, width + rq, jnp.where((rq >= ROWS) & (rq < ROWS + HALO), rq - ROWS - HALO, FAR))
    rim_w, sum_w = [], []
    for a in range(angles):
        hi, lo = two_taps(rcol - rt == off[a], rcol - rt == off[a] + 1, frac[a])
        rim_w.append((jnp.concatenate([hi.astype(F32), lo.astype(F32)], axis=0).astype(BF16), hi))
        sum_w.append(jnp.where((rq == HALO + a) | (rq == ROWS + HALO + a), 1.0, 0.0).astype(BF16))

    wq = iota((ROWS, width), 0)
    wu = iota((ROWS, width), 1)
    w_hi, w_lo = [], []
    for x in range(nx):
        for al in range(na):
            place = jnp.where(me_x == x + 1, wq, jnp.where(me_x == x - 1, width - HALO + wq, FAR))
            val = jnp.where((wq < HALO) & (place == wu), 1.0, 0.0)
            for a in range(angles):
                o = pabuf[al, 3 * a : 3 * a + 1, 0:1]
                fr = pabuf[al, 3 * a + 1 : 3 * a + 2, 0:1]
                sd = pabuf[al, 3 * a + 2 : 3 * a + 3, 0:1]
                t0 = (wu + me_x * width).astype(F32) - o

                def sees(tt):
                    above = (tt >= (x + 1) * width) & (tt < trans_total)
                    below = (tt < x * width) & (tt >= 0)
                    return jnp.where(sd > 0.5, jnp.where(above, 1.0, 0.0), jnp.where(below, 1.0, 0.0))

                both = (1.0 - fr) * sees(t0) + fr * sees(t0 - 1.0)
                val = jnp.where(wq == HALO + a, both, val)
            hi = val.astype(BF16).astype(F32)
            w_hi.append(hi)
            w_lo.append(val - hi)
    fold_w = stack_w(jnp.concatenate(w_hi, axis=0), jnp.concatenate(w_lo, axis=0))

    for kh in range(na):
        h = lax.rem(me_a + 1 + kh, na)
        for b in peers(me_b, nb):
            arrive(pbuf.at[b, h], ps_s.at[h * nb + b], pr_s.at[h * nb + b])
        full = pbuf[0, h]
        down = jnp.where(0 > me_b, full, 0.0)
        for b in range(1, nb):
            full = full + pbuf[b, h]
            down = down + jnp.where(b > me_b, pbuf[b, h], 0.0)
        missed = []
        for a in range(angles):
            for s in range(share):
                row = (a * share + s) * elems
                m = full[row : row + elems] - meas[a, h * share + s]
                res[a, h * share + s] = m
                missed.append(m)
        m_all = jnp.concatenate(missed, axis=0)
        later_all = m_all * down
        gext = None
        msg = None
        for a in range(angles):
            def per_slice(rows_of):
                return jnp.concatenate(
                    [jnp.broadcast_to(rows_of(s), (cells, width)) for s in range(share)], axis=0)

            later = per_slice(lambda s: jnp.sum(
                later_all[(a * share + s) * elems : (a * share + s + 1) * elems], axis=0, keepdims=True))
            direct, prod = [], []
            for e in range(elems):
                me = per_slice(lambda s: m_all[(a * share + s) * elems + e : (a * share + s) * elems + e + 1])
                direct.append(me * wt[h, a, e])
                prod.append(me * wsd[h, a, e])
            s_hi, s_lo = split(sum(prod))
            ga = -dxb * (nn(high, s_hi) + nn(high, s_lo) + later)
            mix = jnp.concatenate(
                [sum((-dxt * kfl[e, f]) * prod[e] for e in range(elems)) for f in range(elems)], axis=0)
            x_hi, x_lo = split(mix)
            back = nt(x_hi, tri[a]) + nt(x_lo, tri[a])
            gs = jnp.concatenate(
                [direct[f] + kinc[f] * ga + back[f * unit : (f + 1) * unit] for f in range(elems)], axis=0)
            g_hi, g_lo = split(gs)
            own = (slice(0, width), slice(None))
            term = nt(g_hi, m_hi[a, :width]) + nt(g_lo, m_hi[a, :width]) + nt(g_hi, m_lo[a, :width])
            gext = term if gext is None else gext + term
            first = nt(rim_w[a][0], g_hi)
            mm = first[: 2 * ROWS] + first[2 * ROWS :] + nt(rim_w[a][1], g_lo)
            mm = mm + nt(sum_w[a], x_hi) + nt(sum_w[a], x_lo)
            msg = mm if msg is None else msg + mm
        gmain[h] = gext
        rsend[h] = msg
        if kh < na - 1:
            sent.append(send(gmain.at[h], mrecv.at[me_a], ms_s.at[h], mr_s.at[me_a], dev(me_b, h, me_x)))
        for kx in range(nx):
            x = lax.rem(me_x + kx, nx)
            if kx == 0 and kh == na - 1:
                continue
            part = pl.multiple_of(jnp.where(x >= me_x, 0, ROWS), ROWS)
            slot = me_x * na + me_a
            sent.append(send(rsend.at[h, pl.ds(part, ROWS)], rbuf.at[slot], rs_s.at[h * nx + x], rr_s.at[slot], dev(me_b, h, x)))
    rbuf[me_x * na + me_a] = rsend[me_a, :ROWS]

    total = gmain[me_a]
    for a in peers(me_a, na):
        arrive(mrecv.at[a], ms_s.at[a], mr_s.at[a])
        total = total + mrecv[a]
    for ka in range(na):
        for kx in range(nx):
            if ka or kx:
                i = lax.rem(me_x + kx, nx) * na + lax.rem(me_a + ka, na)
                arrive(rbuf.at[i], rs_s.at[0], rr_s.at[i])
    rall = jnp.concatenate([rbuf[i] for i in range(nx * na)], axis=0)
    total = total + nn(stack_t(rall), fold_w)
    step = 8.0 * beam_total / (angles * na)
    for f in range(elems):
        new = dens[f, pl.ds(me_a * share, share)].reshape(unit, width) - step * total[f * unit : (f + 1) * unit]
        upd[f] = new.reshape(share, cells, width)
    for copy in sent:
        copy.wait_send()


def local(sizes, density, measured, offsets, sides, shear_frac, k_incident, k_fluor):
    nb, na, nx = sizes
    elems, slices, cells, width = density.shape
    angles = measured.shape[0]
    share = slices // na
    unit = share * cells
    rows_h = elems * unit
    vm = pl.BlockSpec(memory_space=pltpu.VMEM)
    sm = pl.BlockSpec(memory_space=pltpu.SMEM)
    dma = pltpu.SemaphoreType.DMA
    return pl.pallas_call(
        functools.partial(kernel, sizes),
        out_shape=(
            jax.ShapeDtypeStruct((elems, share, cells, width), F32),
            jax.ShapeDtypeStruct(measured.shape, F32),
        ),
        in_specs=[vm, vm, sm, sm, sm, sm, sm],
        out_specs=(vm, vm),
        scratch_shapes=[
            pltpu.VMEM((2 * ROWS, na * rows_h), F32),
            pltpu.VMEM((nx, ROWS, na * rows_h), F32),
            pltpu.VMEM((nb * nx, 2 * slices, width // 2), F32),
            pltpu.VMEM((nb, na, angles * share * elems, width), F32),
            pltpu.VMEM((na, ROWS, 128), F32),
            pltpu.VMEM((na, angles, elems, unit, width), F32),
            pltpu.VMEM((na, angles, elems, unit, width), F32),
            pltpu.VMEM((na, 2 * ROWS, rows_h), F32),
            pltpu.VMEM((nx * na, ROWS, rows_h), F32),
            pltpu.VMEM((na, rows_h, width), F32),
            pltpu.VMEM((na, rows_h, width), F32),
            pltpu.VMEM((angles, width + 128, width), BF16),
            pltpu.VMEM((angles, width + 128, width), BF16),
            pltpu.VMEM((angles, width, width), BF16),
            dma((nx,)), dma((nx,)),
            dma((nb * nx,)), dma((nb * nx,)),
            dma((na * nb,)), dma((na * nb,)),
            dma((na,)), dma((na,)),
            dma((na,)), dma((na,)),
            dma((na * nx,)), dma((na * nx,)),
        ],
        compiler_params=pltpu.CompilerParams(
            collective_id=0, has_side_effects=True, vmem_limit_bytes=40 * 1024 * 1024
        ),
    )(density, measured, offsets, sides, shear_frac, k_incident, k_fluor)


def solution(mesh):
    sizes = (mesh.shape["beam"], mesh.shape["angle"], mesh.shape["trans"])
    return jax.shard_map(
        functools.partial(local, sizes),
        mesh=mesh,
        in_specs=(
            P(None, "groups", "beam", "trans"),
            P("angle", "groups", None, "trans"),
            P("angle"),
            P("angle"),
            P("angle"),
            P(),
            P(),
        ),
        out_specs=(
            P(None, ("groups", "angle"), "beam", "trans"),
            P("angle", "groups", None, "trans"),
        ),
        check_vma=False,
    )
```

```python
import functools

import jax
import jax.numpy as jnp
from jax import lax
from jax.experimental import pallas as pl
from jax.experimental.pallas import tpu as pltpu
from jax.sharding import PartitionSpec as P

F32 = jnp.float32
BF16 = jnp.bfloat16
FAR = 1 << 20
HALO = 4
ROWS = 8


def split(x):
    hi = x.astype(BF16)
    return hi, (x - hi.astype(F32)).astype(BF16)


def nn(a, b):
    return lax.dot_general(a, b, (((1,), (0,)), ((), ())), preferred_element_type=F32)


def nt(a, b):
    return lax.dot_general(a, b, (((1,), (1,)), ((), ())), preferred_element_type=F32)


def iota(shape, dim):
    return lax.broadcasted_iota(jnp.int32, shape, dim)


def two_taps(at_zero, at_one, frac):
    keep = jnp.full((1, at_zero.shape[1]), 1.0 - frac, F32)
    take = jnp.full((1, at_zero.shape[1]), frac, F32)
    keep_hi = keep.astype(BF16).astype(F32)
    take_hi = take.astype(BF16).astype(F32)
    hi = jnp.where(at_zero, keep_hi, jnp.where(at_one, take_hi, 0.0))
    lo = jnp.where(at_zero, keep - keep_hi, jnp.where(at_one, take - take_hi, 0.0))
    return hi.astype(BF16), lo.astype(BF16)


def stack_t(x):
    hi = x.astype(BF16).astype(F32)
    rows = x.shape[0]
    full = -(-3 * rows // 128) * 128
    parts = [hi, x - hi, hi]
    if full > 3 * rows:
        parts.append(jnp.zeros((full - 3 * rows, x.shape[1]), F32))
    return jnp.transpose(jnp.concatenate(parts, axis=0)).astype(BF16)


def stack_w(hi, lo):
    rows = hi.shape[0]
    full = -(-3 * rows // 128) * 128
    parts = [hi.astype(F32), hi.astype(F32), lo.astype(F32)]
    if full > 3 * rows:
        parts.append(jnp.zeros((full - 3 * rows, hi.shape[1]), F32))
    return jnp.concatenate(parts, axis=0).astype(BF16)


def kernel(sizes, dens_in, meas_in, offs_in, sides_in, fracs_in, kinc_in, kfl_in, upd_out, res_out,
           dens, meas, offs, sides, fracs, kinc, kfl, in_s, upd, res, out_s,
           gsend, gbuf, kbuf, pbuf, pabuf, wt, wsd, rsend, rbuf, gmain, mrecv,
           m_hi, m_lo, car, tri, gs_s, gr_s, ks_s, kr_s, ps_s, pr_s, as_s, ar_s, ms_s, mr_s, rs_s, rr_s):
    loads = []
    pairs = ((offs_in, offs), (sides_in, sides), (fracs_in, fracs), (kinc_in, kinc), (kfl_in, kfl),
             (dens_in, dens), (meas_in, meas))
    for i, (src, dst) in enumerate(pairs):
        loads.append(pltpu.make_async_copy(src, dst, in_s.at[i]))
        loads[-1].start()
    nb, na, nx = sizes
    elems, slices, cells, width = dens.shape
    angles = meas.shape[0]
    share = slices // na
    unit = share * cells
    rows_h = elems * unit
    beam_total = cells * nb
    trans_total = width * nx
    dxb = 0.5 / beam_total
    dxt = 0.5 / trans_total
    half = width // 2
    grp = lax.axis_index("groups")
    me_b = lax.axis_index("beam")
    me_a = lax.axis_index("angle")
    me_x = lax.axis_index("trans")

    def dev(b, a, x):
        return (grp, b, a, x)

    def peers(me, count):
        return [lax.rem(me + k, count) for k in range(1, count)]

    barrier = pltpu.get_barrier_semaphore()
    greeted = 0
    for kb in range(nb):
        for kx in range(nx):
            if kb or kx:
                pl.semaphore_signal(barrier, inc=1, device_id_type=pl.DeviceIdType.MESH,
                                    device_id=dev(lax.rem(me_b + kb, nb), me_a, lax.rem(me_x + kx, nx)))
                greeted += 1
    for ka in range(1, na):
        for kx in range(nx):
            pl.semaphore_signal(barrier, inc=1, device_id_type=pl.DeviceIdType.MESH,
                                device_id=dev(me_b, lax.rem(me_a + ka, na), lax.rem(me_x + kx, nx)))
            greeted += 1

    def send(src, dst, ssem, rsem, to):
        copy = pltpu.make_async_remote_copy(src_ref=src, dst_ref=dst, send_sem=ssem, recv_sem=rsem,
                                            device_id=to, device_id_type=pl.DeviceIdType.MESH)
        copy.start()
        return copy

    def arrive(dst, ssem, rsem):
        pltpu.make_async_remote_copy(src_ref=dst, dst_ref=dst, send_sem=ssem, recv_sem=rsem,
                                     device_id=dev(me_b, me_a, me_x),
                                     device_id_type=pl.DeviceIdType.MESH).wait_recv()

    for copy in loads[:5]:
        copy.wait()
    sent = []
    off = [offs[a] for a in range(angles)]
    side = [sides[a] for a in range(angles)]
    frac = [fracs[a] for a in range(angles)]

    def dens_rows(h, e):
        return dens[e, pl.ds(h * share, share)].reshape(unit, width)

    q = iota((2 * ROWS, width), 0)
    u = iota((2 * ROWS, width), 1)
    up = q < ROWS
    qq = jnp.where(up, q, q - ROWS)
    pick = jnp.where((qq < HALO) & (jnp.where(up, width - HALO + qq, qq) == u), 1.0, 0.0)
    e_hi, e_lo = pick.astype(BF16).astype(F32), jnp.zeros_like(pick)

    def counted(t):
        inside = (t + me_x * width >= 0) & (t + me_x * width < trans_total)
        kept = jnp.where(up, t, width - 1 - t) < width
        return kept & inside, jnp.logical_not(kept) & inside

    for a in range(angles):
        t0 = u - off[a]
        in0, out0 = counted(t0)
        in1, out1 = counted(t0 - 1)
        keep = jnp.full((1, width), 1.0 - frac[a], F32)
        take = jnp.full((1, width), frac[a], F32)
        val_in = jnp.where(in0, keep, 0.0) + jnp.where(in1, take, 0.0)
        val_out = jnp.where(out0, keep, 0.0) + jnp.where(out1, take, 0.0)
        val = jnp.where(qq == HALO + a, val_in, jnp.where(qq == HALO + angles + a, val_out, 0.0))
        val_hi = val.astype(BF16).astype(F32)
        e_hi = e_hi + val_hi
        e_lo = e_lo + (val - val_hi)
    e_both = jnp.concatenate([e_hi, e_lo], axis=0).astype(BF16)
    e_hi = e_hi.astype(BF16)

    loads[5].wait()
    total = sum(kinc[e] * dens[e] for e in range(elems))
    ksum = jnp.sum(total, axis=1)
    k8 = jnp.concatenate([ksum[:, :half], ksum[:, half:]], axis=0)
    kbuf[me_b * nx + me_x] = k8
    dhl = []
    order = [lax.rem(me_a + 1 + kh, na) for kh in range(na)]
    for h in order:
        d = jnp.concatenate([dens_rows(h, e) for e in range(elems)], axis=0)
        d_hi, d_lo = split(d)
        dhl.append((d_hi, d_lo))
        first = nt(e_both, d_hi)
        msg = first[: 2 * ROWS] + first[2 * ROWS :] + nt(e_hi, d_lo)
        gsend[:, pl.ds(pl.multiple_of(h * rows_h, rows_h), rows_h)] = msg
    prm = iota((ROWS, 128), 0)
    tile = jnp.zeros((ROWS, 128), F32)
    for a in range(angles):
        tile = jnp.where(prm == 3 * a, off[a].astype(F32), tile)
        tile = jnp.where(prm == 3 * a + 1, frac[a], tile)
        tile = jnp.where(prm == 3 * a + 2, side[a].astype(F32), tile)
    pabuf[me_a] = tile

    pl.semaphore_wait(barrier, greeted)
    for x in peers(me_x, nx):
        part = pl.multiple_of(jnp.where(x > me_x, 0, ROWS), ROWS)
        sent.append(send(gsend.at[pl.ds(part, ROWS)], gbuf.at[me_x], gs_s.at[x], gr_s.at[me_x], dev(me_b, me_a, x)))
    for kb in range(1, nb):
        for kx in range(nx):
            b, x = lax.rem(me_b + kb, nb), lax.rem(me_x + kx, nx)
            own = kbuf.at[me_b * nx + me_x]
            sent.append(send(own, own, ks_s.at[b * nx + x], kr_s.at[me_b * nx + me_x], dev(b, me_a, x)))
    for a in peers(me_a, na):
        own = pabuf.at[me_a]
        sent.append(send(own, own, as_s.at[a], ar_s.at[me_a], dev(me_b, a, me_x)))

    k = iota((width + 128, width), 0)
    t = iota((width + 128, width), 1)
    col = jnp.where(k < width + 64, k, k - width - 128)
    d0 = col - t
    td = iota((width, width), 0) - iota((width, width), 1)
    for a in range(angles):
        hi, lo = two_taps(d0 == off[a], d0 == off[a] + 1, frac[a])
        m_hi[a] = hi
        m_lo[a] = lo
        sgn = jnp.where(side[a] == 1, 1, -1)
        tri[a] = jnp.where(td == 0, 0.5, jnp.where(td * sgn > 0, 1.0, 0.0)).astype(BF16)
    r0 = iota((unit, unit), 0)
    r1 = iota((unit, unit), 1)
    same = (r0 // cells) == (r1 // cells)
    low = jnp.where(r0 == r1, 0.5, jnp.where(same & (r1 < r0), 1.0, 0.0)).astype(BF16)
    high = jnp.where(r0 == r1, 0.5, jnp.where(same & (r1 > r0), 1.0, 0.0)).astype(BF16)
    g = iota((ROWS * nx, width), 0)
    gt = iota((ROWS * nx, width), 1)
    gx = g // ROWS
    gq = g - gx * ROWS
    gcol = jnp.where(gx == me_x + 1, width + gq, jnp.where(gx == me_x - 1, gq - HALO, FAR))
    gcol = jnp.where(gq < HALO, gcol, FAR)
    halo_w = []
    for a in range(angles):
        hi, lo = two_taps(gcol - gt == off[a], gcol - gt == off[a] + 1, frac[a])
        seen = jnp.where(side[a] == 1, gx - me_x, me_x - gx)
        use = ((gq == HALO + a) & (seen > 0)) | ((gq == HALO + angles + a) & ((seen == 0) | (seen > 1)))
        ca = jnp.where(use, 1.0, 0.0).astype(BF16)
        halo_w.append((stack_w(hi, lo), stack_w(ca, jnp.zeros_like(ca))))

    sheared0 = [[nn(dhl[h][0], m_hi[a, :width]) + nn(dhl[h][1], m_hi[a, :width]) + nn(dhl[h][0], m_lo[a, :width])
                 for a in range(angles)] for h in range(na)]

    spill = gsend[...]
    own_slot = spill[:ROWS]
    sq = iota((ROWS, spill.shape[1]), 0)
    for a in range(angles):
        pick_up = jnp.where(side[a] == 1, 1, 0)
        chosen = jnp.where((sq == HALO + angles + a) & (pick_up == 0), spill[ROWS:], own_slot)
        own_slot = chosen
    gbuf[me_x] = own_slot

    for x in peers(me_x, nx):
        arrive(gbuf.at[x], gs_s.at[x], gr_s.at[x])
    for kb in range(1, nb):
        for kx in range(nx):
            i = lax.rem(me_b + kb, nb) * nx + lax.rem(me_x + kx, nx)
            arrive(kbuf.at[i], ks_s.at[i], kr_s.at[i])

    ups = []
    for x in range(nx):
        acc = jnp.zeros((2 * slices, half), F32)
        for b in range(nb):
            acc = acc + jnp.where(b < me_b, kbuf[b * nx + x], 0.0)
        ups.append(acc)
    own_up = sum(jnp.where(me_x == x, ups[x], 0.0) for x in range(nx))
    right = sum(jnp.where(me_x + 1 == x, ups[x], 0.0) for x in range(nx))
    left = sum(jnp.where(me_x - 1 == x, ups[x], 0.0) for x in range(nx))
    lane = iota((slices, half), 1)
    rim = jnp.where(lane < 64, right[:slices], left[slices:])
    kext = jnp.concatenate([own_up[:slices], own_up[slices:], rim], axis=1)
    kext = jnp.concatenate([kext, jnp.zeros_like(kext)], axis=0)
    k_hi, k_lo = split(kext)
    for a in range(angles):
        car[a] = nn(k_hi, m_hi[a]) + nn(k_lo, m_hi[a]) + nn(k_hi, m_lo[a])


    def spread_rows(a, h):
        return jnp.concatenate(
            [jnp.broadcast_to(car[a, pl.ds(h * share + s, 1)], (cells, width)) for s in range(share)], axis=0)

    for kh, h in enumerate(order):
        cols = pl.ds(pl.multiple_of(h * rows_h, rows_h), rows_h)
        gh = stack_t(jnp.concatenate([gbuf[x, :, cols] for x in range(nx)], axis=0))
        for a in range(angles):
            x = sheared0[kh][a] + nn(gh, halo_w[a][0])
            x_hi, x_lo = split(x)
            raw = nn(x_hi, tri[a]) + nn(x_lo, tri[a]) + nn(gh, halo_w[a][1])
            atten = sum(kinc[e] * x[e * unit : (e + 1) * unit] for e in range(elems))
            a_hi, a_lo = split(atten)
            inc = dxb * (nn(low, a_hi) + nn(low, a_lo) + spread_rows(a, h))
            for e in range(elems):
                path = inc
                for f in range(elems):
                    path = path + (dxt * kfl[e, f]) * raw[f * unit : (f + 1) * unit]
                w = dxb * jnp.exp(-path)
                ws = w * x[e * unit : (e + 1) * unit]
                wt[h, a, e] = w
                wsd[h, a, e] = ws
                part = jnp.sum(ws.reshape(share, cells, width), axis=1)
                for s in range(share):
                    row = (a * share + s) * elems + e
                    pbuf[me_b, h, row : row + 1] = part[s : s + 1]
        for b in peers(me_b, nb):
            own = pbuf.at[me_b, h]
            sent.append(send(own, own, ps_s.at[h * nb + b], pr_s.at[h * nb + me_b], dev(b, me_a, me_x)))

    for a in peers(me_a, na):
        arrive(pabuf.at[a], as_s.at[a], ar_s.at[a])
    rq = iota((2 * ROWS, width), 0)
    rt = iota((2 * ROWS, width), 1)
    rcol = jnp.where(rq < HALO, width + rq, jnp.where((rq >= ROWS) & (rq < ROWS + HALO), rq - ROWS - HALO, FAR))
    rim_w, sum_w = [], []
    for a in range(angles):
        hi, lo = two_taps(rcol - rt == off[a], rcol - rt == off[a] + 1, frac[a])
        rim_w.append((jnp.concatenate([hi.astype(F32), lo.astype(F32)], axis=0).astype(BF16), hi))
        sum_w.append(jnp.where((rq == HALO + a) | (rq == ROWS + HALO + a), 1.0, 0.0).astype(BF16))

    wq = iota((ROWS, width), 0)
    wu = iota((ROWS, width), 1)
    w_hi, w_lo = [], []
    for x in range(nx):
        for al in range(na):
            place = jnp.where(me_x == x + 1, wq, jnp.where(me_x == x - 1, width - HALO + wq, FAR))
            val = jnp.where((wq < HALO) & (place == wu), 1.0, 0.0)
            for a in range(angles):
                o = pabuf[al, 3 * a : 3 * a + 1, 0:1]
                fr = pabuf[al, 3 * a + 1 : 3 * a + 2, 0:1]
                sd = pabuf[al, 3 * a + 2 : 3 * a + 3, 0:1]
                t0 = (wu + me_x * width).astype(F32) - o

                def sees(tt):
                    above = (tt >= (x + 1) * width) & (tt < trans_total)
                    below = (tt < x * width) & (tt >= 0)
                    return jnp.where(sd > 0.5, jnp.where(above, 1.0, 0.0), jnp.where(below, 1.0, 0.0))

                both = (1.0 - fr) * sees(t0) + fr * sees(t0 - 1.0)
                val = jnp.where(wq == HALO + a, both, val)
            hi = val.astype(BF16).astype(F32)
            w_hi.append(hi)
            w_lo.append(val - hi)
    fold_w = stack_w(jnp.concatenate(w_hi, axis=0), jnp.concatenate(w_lo, axis=0))

    loads[6].wait()
    for kh, h in enumerate(order):
        for b in peers(me_b, nb):
            arrive(pbuf.at[b, h], ps_s.at[h * nb + b], pr_s.at[h * nb + b])
        full = pbuf[0, h]
        down = jnp.where(0 > me_b, full, 0.0)
        for b in range(1, nb):
            full = full + pbuf[b, h]
            down = down + jnp.where(b > me_b, pbuf[b, h], 0.0)
        missed = []
        for a in range(angles):
            for s in range(share):
                row = (a * share + s) * elems
                m = full[row : row + elems] - meas[a, h * share + s]
                res[a, h * share + s] = m
                missed.append(m)
        m_all = jnp.concatenate(missed, axis=0)
        later_all = m_all * down
        gext = None
        msg = None
        for a in range(angles):
            def per_slice(rows_of):
                return jnp.concatenate(
                    [jnp.broadcast_to(rows_of(s), (cells, width)) for s in range(share)], axis=0)

            later = per_slice(lambda s: jnp.sum(
                later_all[(a * share + s) * elems : (a * share + s + 1) * elems], axis=0, keepdims=True))
            direct, prod = [], []
            for e in range(elems):
                me = per_slice(lambda s: m_all[(a * share + s) * elems + e : (a * share + s) * elems + e + 1])
                direct.append(me * wt[h, a, e])
                prod.append(me * wsd[h, a, e])
            s_hi, s_lo = split(sum(prod))
            ga = -dxb * (nn(high, s_hi) + nn(high, s_lo) + later)
            mix = jnp.concatenate(
                [sum((-dxt * kfl[e, f]) * prod[e] for e in range(elems)) for f in range(elems)], axis=0)
            x_hi, x_lo = split(mix)
            back = nt(x_hi, tri[a]) + nt(x_lo, tri[a])
            gs = jnp.concatenate(
                [direct[f] + kinc[f] * ga + back[f * unit : (f + 1) * unit] for f in range(elems)], axis=0)
            g_hi, g_lo = split(gs)
            term = nt(g_hi, m_hi[a, :width]) + nt(g_lo, m_hi[a, :width]) + nt(g_hi, m_lo[a, :width])
            gext = term if gext is None else gext + term
            first = nt(rim_w[a][0], g_hi)
            mm = first[: 2 * ROWS] + first[2 * ROWS :] + nt(rim_w[a][1], g_lo)
            mm = mm + nt(sum_w[a], x_hi) + nt(sum_w[a], x_lo)
            msg = mm if msg is None else msg + mm
        gmain[h] = gext
        rsend[h] = msg
        if kh < na - 1:
            sent.append(send(gmain.at[h], mrecv.at[me_a], ms_s.at[h], mr_s.at[me_a], dev(me_b, h, me_x)))
        for kx in range(nx):
            x = lax.rem(me_x + kx, nx)
            if kx == 0 and kh == na - 1:
                continue
            part = pl.multiple_of(jnp.where(x >= me_x, 0, ROWS), ROWS)
            slot = me_x * na + me_a
            sent.append(send(rsend.at[h, pl.ds(part, ROWS)], rbuf.at[slot], rs_s.at[h * nx + x], rr_s.at[slot], dev(me_b, h, x)))
    rbuf[me_x * na + me_a] = rsend[me_a, :ROWS]

    stores = [pltpu.make_async_copy(res, res_out, out_s.at[elems])]
    stores[0].start()
    total = gmain[me_a]
    for a in peers(me_a, na):
        arrive(mrecv.at[a], ms_s.at[a], mr_s.at[a])
        total = total + mrecv[a]
    for ka in range(na):
        for kx in range(nx):
            if ka or kx:
                i = lax.rem(me_x + kx, nx) * na + lax.rem(me_a + ka, na)
                arrive(rbuf.at[i], rs_s.at[0], rr_s.at[i])
    rall = jnp.concatenate([rbuf[i] for i in range(nx * na)], axis=0)
    total = total + nn(stack_t(rall), fold_w)
    step = 8.0 * beam_total / (angles * na)
    for f in range(elems):
        new = dens[f, pl.ds(me_a * share, share)].reshape(unit, width) - step * total[f * unit : (f + 1) * unit]
        upd[f] = new.reshape(share, cells, width)
        stores.append(pltpu.make_async_copy(upd.at[f], upd_out.at[f], out_s.at[f]))
        stores[-1].start()
    for copy in sent:
        copy.wait_send()
    for copy in stores:
        copy.wait()


def local(sizes, density, measured, offsets, sides, shear_frac, k_incident, k_fluor):
    nb, na, nx = sizes
    elems, slices, cells, width = density.shape
    angles = measured.shape[0]
    share = slices // na
    unit = share * cells
    rows_h = elems * unit
    hbm = pl.BlockSpec(memory_space=pl.ANY)
    dma = pltpu.SemaphoreType.DMA
    return pl.pallas_call(
        functools.partial(kernel, sizes),
        out_shape=(
            jax.ShapeDtypeStruct((elems, share, cells, width), F32),
            jax.ShapeDtypeStruct(measured.shape, F32),
        ),
        in_specs=[hbm] * 7,
        out_specs=(hbm, hbm),
        scratch_shapes=[
            pltpu.VMEM(density.shape, F32),
            pltpu.VMEM(measured.shape, F32),
            pltpu.SMEM(offsets.shape, jnp.int32),
            pltpu.SMEM(sides.shape, jnp.int32),
            pltpu.SMEM(shear_frac.shape, F32),
            pltpu.SMEM(k_incident.shape, F32),
            pltpu.SMEM(k_fluor.shape, F32),
            dma((7,)),
            pltpu.VMEM((elems, share, cells, width), F32),
            pltpu.VMEM(measured.shape, F32),
            dma((elems + 1,)),
            pltpu.VMEM((2 * ROWS, na * rows_h), F32),
            pltpu.VMEM((nx, ROWS, na * rows_h), F32),
            pltpu.VMEM((nb * nx, 2 * slices, width // 2), F32),
            pltpu.VMEM((nb, na, angles * share * elems, width), F32),
            pltpu.VMEM((na, ROWS, 128), F32),
            pltpu.VMEM((na, angles, elems, unit, width), F32),
            pltpu.VMEM((na, angles, elems, unit, width), F32),
            pltpu.VMEM((na, 2 * ROWS, rows_h), F32),
            pltpu.VMEM((nx * na, ROWS, rows_h), F32),
            pltpu.VMEM((na, rows_h, width), F32),
            pltpu.VMEM((na, rows_h, width), F32),
            pltpu.VMEM((angles, width + 128, width), BF16),
            pltpu.VMEM((angles, width + 128, width), BF16),
            pltpu.VMEM((angles, 2 * slices, width), F32),
            pltpu.VMEM((angles, width, width), BF16),
            dma((nx,)), dma((nx,)),
            dma((nb * nx,)), dma((nb * nx,)),
            dma((na * nb,)), dma((na * nb,)),
            dma((na,)), dma((na,)),
            dma((na,)), dma((na,)),
            dma((na * nx,)), dma((na * nx,)),
        ],
        compiler_params=pltpu.CompilerParams(
            collective_id=0, has_side_effects=True, vmem_limit_bytes=64 * 1024 * 1024
        ),
    )(density, measured, offsets, sides, shear_frac, k_incident, k_fluor)


def solution(mesh):
    sizes = (mesh.shape["beam"], mesh.shape["angle"], mesh.shape["trans"])
    return jax.shard_map(
        functools.partial(local, sizes),
        mesh=mesh,
        in_specs=(
            P(None, "groups", "beam", "trans"),
            P("angle", "groups", None, "trans"),
            P("angle"),
            P("angle"),
            P("angle"),
            P(),
            P(),
        ),
        out_specs=(
            P(None, ("groups", "angle"), "beam", "trans"),
            P("angle", "groups", None, "trans"),
        ),
        check_vma=False,
    )
```

```python
import functools

import jax
import jax.numpy as jnp
from jax import lax
from jax.experimental import pallas as pl
from jax.experimental.pallas import tpu as pltpu
from jax.sharding import PartitionSpec as P

F32 = jnp.float32
BF16 = jnp.bfloat16
FAR = 1 << 20
HALO = 4
ROWS = 8


def split(x):
    hi = x.astype(BF16)
    return hi, (x - hi.astype(F32)).astype(BF16)


def nn(a, b):
    return lax.dot_general(a, b, (((1,), (0,)), ((), ())), preferred_element_type=F32)


def nt(a, b):
    return lax.dot_general(a, b, (((1,), (1,)), ((), ())), preferred_element_type=F32)


def iota(shape, dim):
    return lax.broadcasted_iota(jnp.int32, shape, dim)


def two_taps(at_zero, at_one, frac):
    keep = jnp.full((1, at_zero.shape[1]), 1.0 - frac, F32)
    take = jnp.full((1, at_zero.shape[1]), frac, F32)
    keep_hi = keep.astype(BF16).astype(F32)
    take_hi = take.astype(BF16).astype(F32)
    hi = jnp.where(at_zero, keep_hi, jnp.where(at_one, take_hi, 0.0))
    lo = jnp.where(at_zero, keep - keep_hi, jnp.where(at_one, take - take_hi, 0.0))
    return hi.astype(BF16), lo.astype(BF16)


def stack_t(x):
    hi = x.astype(BF16).astype(F32)
    rows = x.shape[0]
    full = -(-3 * rows // 128) * 128
    parts = [hi, x - hi, hi]
    if full > 3 * rows:
        parts.append(jnp.zeros((full - 3 * rows, x.shape[1]), F32))
    return jnp.transpose(jnp.concatenate(parts, axis=0)).astype(BF16)


def stack_w(hi, lo):
    rows = hi.shape[0]
    full = -(-3 * rows // 128) * 128
    parts = [hi.astype(F32), hi.astype(F32), lo.astype(F32)]
    if full > 3 * rows:
        parts.append(jnp.zeros((full - 3 * rows, hi.shape[1]), F32))
    return jnp.concatenate(parts, axis=0).astype(BF16)


def kernel(sizes, dens_in, meas_in, offs_in, sides_in, fracs_in, kinc_in, kfl_in, upd_out, res_out,
           dens, meas, offs, sides, fracs, kinc, kfl, in_s, upd, res, out_s,
           gsend, gbuf, kbuf, pbuf, pabuf, wt, wsd, rsend, rbuf, gmain, mrecv,
           m_hi, m_lo, car, tri, gs_s, gr_s, ks_s, kr_s, ps_s, pr_s, as_s, ar_s, ms_s, mr_s, rs_s, rr_s):
    loads = []
    pairs = ((offs_in, offs), (sides_in, sides), (fracs_in, fracs), (kinc_in, kinc), (kfl_in, kfl),
             (dens_in, dens), (meas_in, meas))
    for i, (src, dst) in enumerate(pairs):
        loads.append(pltpu.make_async_copy(src, dst, in_s.at[i]))
        loads[-1].start()
    nb, na, nx = sizes
    elems, slices, cells, width = dens.shape
    angles = meas.shape[0]
    share = slices // na
    unit = share * cells
    rows_h = elems * unit
    beam_total = cells * nb
    trans_total = width * nx
    dxb = 0.5 / beam_total
    dxt = 0.5 / trans_total
    half = width // 2
    grp = lax.axis_index("groups")
    me_b = lax.axis_index("beam")
    me_a = lax.axis_index("angle")
    me_x = lax.axis_index("trans")

    def dev(b, a, x):
        return (grp, b, a, x)

    def peers(me, count):
        return [lax.rem(me + k, count) for k in range(1, count)]

    barrier = pltpu.get_barrier_semaphore()
    greeted = 0
    for kb in range(nb):
        for kx in range(nx):
            if kb or kx:
                pl.semaphore_signal(barrier, inc=1, device_id_type=pl.DeviceIdType.MESH,
                                    device_id=dev(lax.rem(me_b + kb, nb), me_a, lax.rem(me_x + kx, nx)))
                greeted += 1
    for ka in range(1, na):
        for kx in range(nx):
            pl.semaphore_signal(barrier, inc=1, device_id_type=pl.DeviceIdType.MESH,
                                device_id=dev(me_b, lax.rem(me_a + ka, na), lax.rem(me_x + kx, nx)))
            greeted += 1

    def send(src, dst, ssem, rsem, to):
        copy = pltpu.make_async_remote_copy(src_ref=src, dst_ref=dst, send_sem=ssem, recv_sem=rsem,
                                            device_id=to, device_id_type=pl.DeviceIdType.MESH)
        copy.start()
        return copy

    def arrive(dst, ssem, rsem):
        pltpu.make_async_remote_copy(src_ref=dst, dst_ref=dst, send_sem=ssem, recv_sem=rsem,
                                     device_id=dev(me_b, me_a, me_x),
                                     device_id_type=pl.DeviceIdType.MESH).wait_recv()

    for copy in loads[:5]:
        copy.wait()
    sent = []
    off = [offs[a] for a in range(angles)]
    side = [sides[a] for a in range(angles)]
    frac = [fracs[a] for a in range(angles)]

    def dens_rows(h, e):
        return dens[e, pl.ds(h * share, share)].reshape(unit, width)

    q = iota((2 * ROWS, width), 0)
    u = iota((2 * ROWS, width), 1)
    up = q < ROWS
    qq = jnp.where(up, q, q - ROWS)
    pick = jnp.where((qq < HALO) & (jnp.where(up, width - HALO + qq, qq) == u), 1.0, 0.0)
    e_hi, e_lo = pick.astype(BF16).astype(F32), jnp.zeros_like(pick)

    def counted(t):
        inside = (t + me_x * width >= 0) & (t + me_x * width < trans_total)
        kept = jnp.where(up, t, width - 1 - t) < width
        return kept & inside, jnp.logical_not(kept) & inside

    for a in range(angles):
        t0 = u - off[a]
        in0, out0 = counted(t0)
        in1, out1 = counted(t0 - 1)
        keep = jnp.full((1, width), 1.0 - frac[a], F32)
        take = jnp.full((1, width), frac[a], F32)
        val_in = jnp.where(in0, keep, 0.0) + jnp.where(in1, take, 0.0)
        val_out = jnp.where(out0, keep, 0.0) + jnp.where(out1, take, 0.0)
        val = jnp.where(qq == HALO + a, val_in, jnp.where(qq == HALO + angles + a, val_out, 0.0))
        val_hi = val.astype(BF16).astype(F32)
        e_hi = e_hi + val_hi
        e_lo = e_lo + (val - val_hi)
    e_both = jnp.concatenate([e_hi, e_lo], axis=0).astype(BF16)
    e_hi = e_hi.astype(BF16)

    loads[5].wait()
    total = sum(kinc[e] * dens[e] for e in range(elems))
    ksum = jnp.sum(total, axis=1)
    k8 = jnp.concatenate([ksum[:, :half], ksum[:, half:]], axis=0)
    kbuf[me_b * nx + me_x] = k8
    dhl = []
    order = [lax.rem(me_a + 1 + kh, na) for kh in range(na)]
    for h in order:
        d = jnp.concatenate([dens_rows(h, e) for e in range(elems)], axis=0)
        d_hi, d_lo = split(d)
        dhl.append((d_hi, d_lo))
        first = nt(e_both, d_hi)
        msg = first[: 2 * ROWS] + first[2 * ROWS :] + nt(e_hi, d_lo)
        gsend[:, pl.ds(pl.multiple_of(h * rows_h, rows_h), rows_h)] = msg
    prm = iota((ROWS, 128), 0)
    tile = jnp.zeros((ROWS, 128), F32)
    for a in range(angles):
        tile = jnp.where(prm == 3 * a, off[a].astype(F32), tile)
        tile = jnp.where(prm == 3 * a + 1, frac[a], tile)
        tile = jnp.where(prm == 3 * a + 2, side[a].astype(F32), tile)
    pabuf[me_a] = tile

    pl.semaphore_wait(barrier, greeted)
    for kb in range(1, nb):
        for kx in range(nx):
            b, x = lax.rem(me_b + kb, nb), lax.rem(me_x + kx, nx)
            own = kbuf.at[me_b * nx + me_x]
            sent.append(send(own, own, ks_s.at[b * nx + x], kr_s.at[me_b * nx + me_x], dev(b, me_a, x)))
    for x in peers(me_x, nx):
        part = pl.multiple_of(jnp.where(x > me_x, 0, ROWS), ROWS)
        sent.append(send(gsend.at[pl.ds(part, ROWS)], gbuf.at[me_x], gs_s.at[x], gr_s.at[me_x], dev(me_b, me_a, x)))
    for a in peers(me_a, na):
        own = pabuf.at[me_a]
        sent.append(send(own, own, as_s.at[a], ar_s.at[me_a], dev(me_b, a, me_x)))

    k = iota((width + 128, width), 0)
    t = iota((width + 128, width), 1)
    col = jnp.where(k < width + 64, k, k - width - 128)
    d0 = col - t
    td = iota((width, width), 0) - iota((width, width), 1)
    for a in range(angles):
        hi, lo = two_taps(d0 == off[a], d0 == off[a] + 1, frac[a])
        m_hi[a] = hi
        m_lo[a] = lo
        sgn = jnp.where(side[a] == 1, 1, -1)
        tri[a] = jnp.where(td == 0, 0.5, jnp.where(td * sgn > 0, 1.0, 0.0)).astype(BF16)
    r0 = iota((unit, unit), 0)
    r1 = iota((unit, unit), 1)
    same = (r0 // cells) == (r1 // cells)
    low = jnp.where(r0 == r1, 0.5, jnp.where(same & (r1 < r0), 1.0, 0.0)).astype(BF16)
    high = jnp.where(r0 == r1, 0.5, jnp.where(same & (r1 > r0), 1.0, 0.0)).astype(BF16)
    g = iota((ROWS * nx, width), 0)
    gt = iota((ROWS * nx, width), 1)
    gx = g // ROWS
    gq = g - gx * ROWS
    gcol = jnp.where(gx == me_x + 1, width + gq, jnp.where(gx == me_x - 1, gq - HALO, FAR))
    gcol = jnp.where(gq < HALO, gcol, FAR)
    halo_w = []
    for a in range(angles):
        hi, lo = two_taps(gcol - gt == off[a], gcol - gt == off[a] + 1, frac[a])
        seen = jnp.where(side[a] == 1, gx - me_x, me_x - gx)
        use = ((gq == HALO + a) & (seen > 0)) | ((gq == HALO + angles + a) & ((seen == 0) | (seen > 1)))
        ca = jnp.where(use, 1.0, 0.0).astype(BF16)
        halo_w.append((stack_w(hi, lo), stack_w(ca, jnp.zeros_like(ca))))

    sheared0 = [[nn(dhl[h][0], m_hi[a, :width]) + nn(dhl[h][1], m_hi[a, :width]) + nn(dhl[h][0], m_lo[a, :width])
                 for a in range(angles)] for h in range(na)]

    spill = gsend[...]
    own_slot = spill[:ROWS]
    sq = iota((ROWS, spill.shape[1]), 0)
    for a in range(angles):
        pick_up = jnp.where(side[a] == 1, 1, 0)
        chosen = jnp.where((sq == HALO + angles + a) & (pick_up == 0), spill[ROWS:], own_slot)
        own_slot = chosen
    gbuf[me_x] = own_slot

    for x in peers(me_x, nx):
        arrive(gbuf.at[x], gs_s.at[x], gr_s.at[x])
    def spread_rows(a, h):
        return jnp.concatenate(
            [jnp.broadcast_to(car[a, pl.ds(h * share + s, 1)], (cells, width)) for s in range(share)], axis=0)

    early = []
    for kh, h in enumerate(order):
        cols = pl.ds(pl.multiple_of(h * rows_h, rows_h), rows_h)
        gh = stack_t(jnp.concatenate([gbuf[x, :, cols] for x in range(nx)], axis=0))
        for a in range(angles):
            x = sheared0[kh][a] + nn(gh, halo_w[a][0])
            x_hi, x_lo = split(x)
            raw = nn(x_hi, tri[a]) + nn(x_lo, tri[a]) + nn(gh, halo_w[a][1])
            atten = sum(kinc[e] * x[e * unit : (e + 1) * unit] for e in range(elems))
            a_hi, a_lo = split(atten)
            early.append((x, raw, nn(low, a_hi) + nn(low, a_lo)))

    for kb in range(1, nb):
        for kx in range(nx):
            i = lax.rem(me_b + kb, nb) * nx + lax.rem(me_x + kx, nx)
            arrive(kbuf.at[i], ks_s.at[i], kr_s.at[i])

    ups = []
    for x in range(nx):
        acc = jnp.zeros((2 * slices, half), F32)
        for b in range(nb):
            acc = acc + jnp.where(b < me_b, kbuf[b * nx + x], 0.0)
        ups.append(acc)
    own_up = sum(jnp.where(me_x == x, ups[x], 0.0) for x in range(nx))
    right = sum(jnp.where(me_x + 1 == x, ups[x], 0.0) for x in range(nx))
    left = sum(jnp.where(me_x - 1 == x, ups[x], 0.0) for x in range(nx))
    lane = iota((slices, half), 1)
    rim = jnp.where(lane < 64, right[:slices], left[slices:])
    kext = jnp.concatenate([own_up[:slices], own_up[slices:], rim], axis=1)
    kext = jnp.concatenate([kext, jnp.zeros_like(kext)], axis=0)
    k_hi, k_lo = split(kext)
    for a in range(angles):
        car[a] = nn(k_hi, m_hi[a]) + nn(k_lo, m_hi[a]) + nn(k_hi, m_lo[a])


    for kh, h in enumerate(order):
        for a in range(angles):
            x, raw, ahead = early[kh * angles + a]
            inc = dxb * (ahead + spread_rows(a, h))
            for e in range(elems):
                path = inc
                for f in range(elems):
                    path = path + (dxt * kfl[e, f]) * raw[f * unit : (f + 1) * unit]
                w = dxb * jnp.exp(-path)
                ws = w * x[e * unit : (e + 1) * unit]
                wt[h, a, e] = w
                wsd[h, a, e] = ws
                part = jnp.sum(ws.reshape(share, cells, width), axis=1)
                for s in range(share):
                    row = (a * share + s) * elems + e
                    pbuf[me_b, h, row : row + 1] = part[s : s + 1]
        for b in peers(me_b, nb):
            own = pbuf.at[me_b, h]
            sent.append(send(own, own, ps_s.at[h * nb + b], pr_s.at[h * nb + me_b], dev(b, me_a, me_x)))

    for a in peers(me_a, na):
        arrive(pabuf.at[a], as_s.at[a], ar_s.at[a])
    rq = iota((2 * ROWS, width), 0)
    rt = iota((2 * ROWS, width), 1)
    rcol = jnp.where(rq < HALO, width + rq, jnp.where((rq >= ROWS) & (rq < ROWS + HALO), rq - ROWS - HALO, FAR))
    rim_w, sum_w = [], []
    for a in range(angles):
        hi, lo = two_taps(rcol - rt == off[a], rcol - rt == off[a] + 1, frac[a])
        rim_w.append((jnp.concatenate([hi.astype(F32), lo.astype(F32)], axis=0).astype(BF16), hi))
        sum_w.append(jnp.where((rq == HALO + a) | (rq == ROWS + HALO + a), 1.0, 0.0).astype(BF16))

    wq = iota((ROWS, width), 0)
    wu = iota((ROWS, width), 1)
    w_hi, w_lo = [], []
    for x in range(nx):
        for al in range(na):
            place = jnp.where(me_x == x + 1, wq, jnp.where(me_x == x - 1, width - HALO + wq, FAR))
            val = jnp.where((wq < HALO) & (place == wu), 1.0, 0.0)
            for a in range(angles):
                o = pabuf[al, 3 * a : 3 * a + 1, 0:1]
                fr = pabuf[al, 3 * a + 1 : 3 * a + 2, 0:1]
                sd = pabuf[al, 3 * a + 2 : 3 * a + 3, 0:1]
                t0 = (wu + me_x * width).astype(F32) - o

                def sees(tt):
                    above = (tt >= (x + 1) * width) & (tt < trans_total)
                    below = (tt < x * width) & (tt >= 0)
                    return jnp.where(sd > 0.5, jnp.where(above, 1.0, 0.0), jnp.where(below, 1.0, 0.0))

                both = (1.0 - fr) * sees(t0) + fr * sees(t0 - 1.0)
                val = jnp.where(wq == HALO + a, both, val)
            hi = val.astype(BF16).astype(F32)
            w_hi.append(hi)
            w_lo.append(val - hi)
    fold_w = stack_w(jnp.concatenate(w_hi, axis=0), jnp.concatenate(w_lo, axis=0))

    loads[6].wait()
    for kh, h in enumerate(order):
        for b in peers(me_b, nb):
            arrive(pbuf.at[b, h], ps_s.at[h * nb + b], pr_s.at[h * nb + b])
        full = pbuf[0, h]
        down = jnp.where(0 > me_b, full, 0.0)
        for b in range(1, nb):
            full = full + pbuf[b, h]
            down = down + jnp.where(b > me_b, pbuf[b, h], 0.0)
        missed = []
        for a in range(angles):
            for s in range(share):
                row = (a * share + s) * elems
                m = full[row : row + elems] - meas[a, h * share + s]
                res[a, h * share + s] = m
                missed.append(m)
        m_all = jnp.concatenate(missed, axis=0)
        later_all = m_all * down
        halves = []
        msg = None
        for a in range(angles):
            def per_slice(rows_of):
                return jnp.concatenate(
                    [jnp.broadcast_to(rows_of(s), (cells, width)) for s in range(share)], axis=0)

            later = per_slice(lambda s: jnp.sum(
                later_all[(a * share + s) * elems : (a * share + s + 1) * elems], axis=0, keepdims=True))
            direct, prod = [], []
            for e in range(elems):
                me = per_slice(lambda s: m_all[(a * share + s) * elems + e : (a * share + s) * elems + e + 1])
                direct.append(me * wt[h, a, e])
                prod.append(me * wsd[h, a, e])
            s_hi, s_lo = split(sum(prod))
            ga = -dxb * (nn(high, s_hi) + nn(high, s_lo) + later)
            mix = jnp.concatenate(
                [sum((-dxt * kfl[e, f]) * prod[e] for e in range(elems)) for f in range(elems)], axis=0)
            x_hi, x_lo = split(mix)
            back = nt(x_hi, tri[a]) + nt(x_lo, tri[a])
            gs = jnp.concatenate(
                [direct[f] + kinc[f] * ga + back[f * unit : (f + 1) * unit] for f in range(elems)], axis=0)
            g_hi, g_lo = split(gs)
            halves.append((g_hi, g_lo))
            first = nt(rim_w[a][0], g_hi)
            mm = first[: 2 * ROWS] + first[2 * ROWS :] + nt(rim_w[a][1], g_lo)
            mm = mm + nt(sum_w[a], x_hi) + nt(sum_w[a], x_lo)
            msg = mm if msg is None else msg + mm
        rsend[h] = msg
        for kx in range(nx):
            x = lax.rem(me_x + kx, nx)
            if kx == 0 and kh == na - 1:
                continue
            part = pl.multiple_of(jnp.where(x >= me_x, 0, ROWS), ROWS)
            slot = me_x * na + me_a
            sent.append(send(rsend.at[h, pl.ds(part, ROWS)], rbuf.at[slot], rs_s.at[h * nx + x], rr_s.at[slot], dev(me_b, h, x)))
        gmain[h] = sum(
            nt(g_hi, m_hi[a, :width]) + nt(g_lo, m_hi[a, :width]) + nt(g_hi, m_lo[a, :width])
            for a, (g_hi, g_lo) in enumerate(halves))
        if kh < na - 1:
            sent.append(send(gmain.at[h], mrecv.at[me_a], ms_s.at[h], mr_s.at[me_a], dev(me_b, h, me_x)))
    rbuf[me_x * na + me_a] = rsend[me_a, :ROWS]

    stores = [pltpu.make_async_copy(res, res_out, out_s.at[elems])]
    stores[0].start()
    total = gmain[me_a]
    for a in peers(me_a, na):
        arrive(mrecv.at[a], ms_s.at[a], mr_s.at[a])
        total = total + mrecv[a]
    for ka in range(na):
        for kx in range(nx):
            if ka or kx:
                i = lax.rem(me_x + kx, nx) * na + lax.rem(me_a + ka, na)
                arrive(rbuf.at[i], rs_s.at[0], rr_s.at[i])
    rall = jnp.concatenate([rbuf[i] for i in range(nx * na)], axis=0)
    total = total + nn(stack_t(rall), fold_w)
    step = 8.0 * beam_total / (angles * na)
    for f in range(elems):
        new = dens[f, pl.ds(me_a * share, share)].reshape(unit, width) - step * total[f * unit : (f + 1) * unit]
        upd[f] = new.reshape(share, cells, width)
        stores.append(pltpu.make_async_copy(upd.at[f], upd_out.at[f], out_s.at[f]))
        stores[-1].start()
    for copy in sent:
        copy.wait_send()
    for copy in stores:
        copy.wait()


def hand_over(new, missed, new_out, missed_out, new_v, missed_v, in_s, out_s):
    elems = new.shape[0]
    legs = [(new.at[f], new_v.at[f], new_out.at[f]) for f in range(elems)]
    legs.append((missed, missed_v, missed_out))
    ins, outs = [], []
    for i, (src, mid, dst) in enumerate(legs):
        ins.append(pltpu.make_async_copy(src, mid, in_s.at[i]))
        outs.append(pltpu.make_async_copy(mid, dst, out_s.at[i]))
        ins[-1].start()
    for arrived, leaving in zip(ins, outs):
        arrived.wait()
        leaving.start()
    for leaving in outs:
        leaving.wait()


def local(sizes, density, measured, offsets, sides, shear_frac, k_incident, k_fluor):
    nb, na, nx = sizes
    elems, slices, cells, width = density.shape
    angles = measured.shape[0]
    share = slices // na
    unit = share * cells
    rows_h = elems * unit
    hbm = pl.BlockSpec(memory_space=pl.ANY)
    dma = pltpu.SemaphoreType.DMA
    new, missed = pl.pallas_call(
        functools.partial(kernel, sizes),
        out_shape=(
            jax.ShapeDtypeStruct((elems, share, cells, width), F32),
            jax.ShapeDtypeStruct(measured.shape, F32),
        ),
        in_specs=[hbm] * 7,
        out_specs=(hbm, hbm),
        scratch_shapes=[
            pltpu.VMEM(density.shape, F32),
            pltpu.VMEM(measured.shape, F32),
            pltpu.SMEM(offsets.shape, jnp.int32),
            pltpu.SMEM(sides.shape, jnp.int32),
            pltpu.SMEM(shear_frac.shape, F32),
            pltpu.SMEM(k_incident.shape, F32),
            pltpu.SMEM(k_fluor.shape, F32),
            dma((7,)),
            pltpu.VMEM((elems, share, cells, width), F32),
            pltpu.VMEM(measured.shape, F32),
            dma((elems + 1,)),
            pltpu.VMEM((2 * ROWS, na * rows_h), F32),
            pltpu.VMEM((nx, ROWS, na * rows_h), F32),
            pltpu.VMEM((nb * nx, 2 * slices, width // 2), F32),
            pltpu.VMEM((nb, na, angles * share * elems, width), F32),
            pltpu.VMEM((na, ROWS, 128), F32),
            pltpu.VMEM((na, angles, elems, unit, width), F32),
            pltpu.VMEM((na, angles, elems, unit, width), F32),
            pltpu.VMEM((na, 2 * ROWS, rows_h), F32),
            pltpu.VMEM((nx * na, ROWS, rows_h), F32),
            pltpu.VMEM((na, rows_h, width), F32),
            pltpu.VMEM((na, rows_h, width), F32),
            pltpu.VMEM((angles, width + 128, width), BF16),
            pltpu.VMEM((angles, width + 128, width), BF16),
            pltpu.VMEM((angles, 2 * slices, width), F32),
            pltpu.VMEM((angles, width, width), BF16),
            dma((nx,)), dma((nx,)),
            dma((nb * nx,)), dma((nb * nx,)),
            dma((na * nb,)), dma((na * nb,)),
            dma((na,)), dma((na,)),
            dma((na,)), dma((na,)),
            dma((na * nx,)), dma((na * nx,)),
        ],
        compiler_params=pltpu.CompilerParams(
            collective_id=0, has_side_effects=True, vmem_limit_bytes=64 * 1024 * 1024
        ),
    )(density, measured, offsets, sides, shear_frac, k_incident, k_fluor)
    return pl.pallas_call(
        hand_over,
        out_shape=(jax.ShapeDtypeStruct(new.shape, F32), jax.ShapeDtypeStruct(missed.shape, F32)),
        in_specs=[hbm] * 2,
        out_specs=(hbm, hbm),
        scratch_shapes=[pltpu.VMEM(new.shape, F32), pltpu.VMEM(missed.shape, F32),
                        dma((elems + 1,)), dma((elems + 1,))],
        compiler_params=pltpu.CompilerParams(vmem_limit_bytes=64 * 1024 * 1024),
    )(new, missed)


def solution(mesh):
    sizes = (mesh.shape["beam"], mesh.shape["angle"], mesh.shape["trans"])
    return jax.shard_map(
        functools.partial(local, sizes),
        mesh=mesh,
        in_specs=(
            P(None, "groups", "beam", "trans"),
            P("angle", "groups", None, "trans"),
            P("angle"),
            P("angle"),
            P("angle"),
            P(),
            P(),
        ),
        out_specs=(
            P(None, ("groups", "angle"), "beam", "trans"),
            P("angle", "groups", None, "trans"),
        ),
        check_vma=False,
    )
```
